512 devices in a mesh: blk: 64 (over z_lo, x, core), col: 8 (over y, z_hi).
Axes of the slice: x: 4, y: 4, z: 16 (z_hi: 2, z_lo: 8; z = z_hi * 8 + z_lo), core: 2. Of those that a mesh axis runs over, the one named last changes fastest.
Arguments:
- word_vectors: float32 [300, 131072], P(None, ('blk', 'col')), may hold values from -0.6 to 0.6
- word_bias: float32 [131072], P(('blk', 'col')), may hold values from -3 to 3
- context_vectors: float32 [300, 131072], P(None, ('blk', 'col')), may hold values from -0.6 to 0.6
- context_bias: float32 [131072], P(('blk', 'col')), may hold values from -3 to 3
- counts: bfloat16 [2, 131072, 2048], P(None, 'blk', 'col'), may hold values from 0.25 to 400
- tile_mask: int32 [2, 1024, 16], P(None, 'blk', 'col'), may hold values 0 or 1
Outputs:
- new_word_vectors: float32 [300, 131072], P(None, ('blk', 'col'))
- new_word_bias: float32 [131072], P(('blk', 'col'))
- new_context_vectors: float32 [300, 131072], P(None, ('blk', 'col'))
- new_context_bias: float32 [131072], P(('blk', 'col'))
The draws below stay inside these ranges and needn't reach their ends.
All inputs are finite; a program needn't handle non-finite values. No bound on the sum of `tile_mask` on one device may be relied on, other than what follows from the above.
Results may differ from the reference program's by a relative error of at most 0.0075.
Values may be sent and summed in bfloat16 or wider, within the bound.
A program may use at most 64 MiB of HBM per device.

```python
import math
import jax
import jax.numpy as jnp
from jax import lax

DIM = 300
ROWS = 2048
TILE = 128
STRATA = 2
WORDS = 131072
CTX = 256
N_BLK = 64
N_COL = 8


def plant(entries, rng, low, top_value):
    dims = entries.shape
    index_at = [jax.random.randint(jax.random.fold_in(rng, axis), (), 0, dims[axis]) for axis in range(len(dims))]
    entries = entries.at[tuple(index_at)].set(low)
    longest = dims.index(max(dims))
    index_at[longest] = (index_at[longest] + 1) % dims[longest]
    return entries.at[tuple(index_at)].set(top_value)


def steps_of(own_key, dims, cuts, least, largest):
    def one(axis_at, shards_of):
        steps = jax.random.uniform(jax.random.fold_in(jax.random.fold_in(own_key, 6), axis_at), (shards_of,), jnp.float32, least / len(cuts), largest / len(cuts))
        return jnp.repeat(jnp.exp(steps), dims[axis_at] // shards_of).reshape((-1,) + (1,) * (len(dims) - axis_at - 1))

    gain = one(*cuts[0])
    for cut in cuts[1:]:
        gain = gain * one(*cut)
    return gain


def gaussian(own_key, extent, spread, bound, split=(), held_as=jnp.bfloat16):
    level = steps_of(own_key, extent, split, -0.22, 0.18) if split else 1.0
    drawn = jax.random.normal(own_key, extent, jnp.float32) * spread * level
    return jnp.minimum(jnp.maximum(drawn, -bound), bound).astype(held_as)


def setup_inputs(seed: int = 0) -> dict:
    key_list = jax.random.split(jax.random.key(seed), 7)
    return {
        "word_vectors": gaussian(key_list[0], (DIM, WORDS), 0.1, 0.6, ((1, 512),), jnp.float32),
        "word_bias": gaussian(key_list[1], (WORDS,), 0.5, 3.0, ((0, 512),), jnp.float32),
        "context_vectors": gaussian(key_list[2], (DIM, WORDS), 0.1, 0.6, ((1, 512),), jnp.float32),
        "context_bias": gaussian(key_list[3], (WORDS,), 0.5, 3.0, ((0, 512),), jnp.float32),
        "counts": jnp.clip(jnp.exp(math.log(400.0) - 7.377759 * jax.random.uniform(key_list[4], (STRATA, WORDS, ROWS), jnp.float32) ** steps_of(key_list[4], (STRATA, WORDS, ROWS), ((1, 64), (2, 8)), -0.2, 0.2)), 0.25, 400.0).astype(jnp.bfloat16),
        "tile_mask": plant((jax.random.randint(key_list[5], (STRATA, WORDS // TILE, ROWS // TILE), 0, 4) < 3).astype(jnp.int32), jax.random.fold_in(key_list[5], 1), 0, 1),
    }


RATE = 0.05
XMAX = 100.0
POWER = 0.75

def adagrad(param, accum, grad):
    accum = accum + grad * grad
    return (param - RATE * grad / jnp.sqrt(accum), accum)

def one_block(items):
    wvec, wbias, wacc, wbacc, cvec, cbias, cacc, cbacc, cnt, msk = items
    xval = cnt.astype(jnp.float32)
    tiles = jnp.repeat(jnp.repeat(msk.astype(jnp.float32), TILE, axis=0), TILE, axis=1)
    weight = tiles * jnp.minimum((xval / XMAX) ** POWER, 1.0)
    target = jnp.log(jnp.maximum(xval, 1.0))
    pred = lax.dot_general(wvec, cvec, (((0,), (0,)), ((), ())), precision=lax.Precision.HIGHEST, preferred_element_type=jnp.float32)
    pred = pred + wbias[:, None] + cbias[None, :]
    grads = weight * (pred - target)
    grouped = grads.reshape(ROWS, N_COL, CTX)
    cgroups = cvec.reshape(DIM, N_COL, CTX)
    parts = jnp.einsum('dkc,rkc->kdr', cgroups, grouped, precision=lax.Precision.HIGHEST)
    grad_word = lax.optimization_barrier(jnp.sum(lax.optimization_barrier(parts.astype(jnp.bfloat16)).astype(jnp.float32), axis=0))
    bparts = lax.optimization_barrier(jnp.sum(grouped, axis=2))
    grad_wbias = lax.optimization_barrier(jnp.sum(lax.optimization_barrier(bparts.astype(jnp.bfloat16)).astype(jnp.float32), axis=1))
    grad_ctx = jnp.dot(wvec, grads, precision=lax.Precision.HIGHEST, preferred_element_type=jnp.float32)
    grad_cbias = lax.optimization_barrier(jnp.sum(grads, axis=0))
    wvec, wacc = adagrad(wvec, wacc, grad_word)
    wbias, wbacc = adagrad(wbias, wbacc, grad_wbias)
    cvec, cacc = adagrad(cvec, cacc, grad_ctx)
    cbias, cbacc = adagrad(cbias, cbacc, grad_cbias)
    return (wvec, wbias, wacc, wbacc, cvec, cbias, cacc, cbacc)

def to_blocks(vectors):
    return vectors.reshape(DIM, N_BLK, ROWS).transpose(1, 0, 2)

def reference(word_vectors, word_bias, context_vectors, context_bias, counts, tile_mask):
    wvec = to_blocks(word_vectors)
    wbias = word_bias.reshape(N_BLK, ROWS)
    cvec = to_blocks(context_vectors)
    cbias = context_bias.reshape(N_BLK, ROWS)
    wacc = jnp.ones_like(wvec)
    wbacc = jnp.ones_like(wbias)
    cacc = jnp.ones_like(cvec)
    cbacc = jnp.ones_like(cbias)
    for stratum in range(STRATA):
        cnt = counts[stratum].reshape(N_BLK, ROWS, ROWS)
        msk = tile_mask[stratum].reshape(N_BLK, ROWS // TILE, ROWS // TILE)
        wvec, wbias, wacc, wbacc, cvec, cbias, cacc, cbacc = lax.map(one_block, (wvec, wbias, wacc, wbacc, cvec, cbias, cacc, cbacc, cnt, msk))
        cvec = jnp.roll(cvec, 1, axis=0)
        cbias = jnp.roll(cbias, 1, axis=0)
        cacc = jnp.roll(cacc, 1, axis=0)
        cbacc = jnp.roll(cbacc, 1, axis=0)
    new_words = wvec.transpose(1, 0, 2).reshape(DIM, WORDS)
    new_context = cvec.transpose(1, 0, 2).reshape(DIM, WORDS)
    return (new_words, wbias.reshape(WORDS), new_context, cbias.reshape(WORDS))
```

```python
import functools
import math

import jax
import jax.numpy as jnp
from jax import lax
from jax.experimental import pallas as pl
from jax.experimental.pallas import tpu as pltpu
from jax.sharding import PartitionSpec as P

RATE = 0.05
XMAX = 100.0
POWER = 0.75
MESH = pl.DeviceIdType.MESH
F32 = jnp.float32
BF16 = jnp.bfloat16
N_Y = 4
SIDE = 128

ORDER = (
    ("prep", 0, 0, 0), ("unit", 0, 0, 0, 0), ("prep", 0, 0, 1), ("unit", 0, 0, 1, 0),
    ("cgrad", 0, 0, 0), ("fwd", 0, 0, 0), ("unit", 0, 0, 0, 1), ("unit", 0, 0, 0, 3),
    ("fwd", 0, 0, 1), ("unit", 0, 0, 1, 1), ("unit", 0, 0, 1, 3), ("cearly",),
    ("unit", 0, 0, 0, 2), ("cgrad", 0, 0, 1), ("cgrad", 0, 0, 3), ("relay", 0, 0),
    ("relay", 0, 1), ("prep", 0, 1, 0), ("prep", 0, 1, 1), ("unit", 0, 0, 1, 2),
    ("cgrad", 0, 0, 2), ("prep", 1, 1, 0), ("prep", 1, 1, 1), ("prep", 1, 0, 0),
    ("prep", 1, 0, 1), ("half", 0, 0, 0), ("half", 0, 0, 1), ("words", 0), ("words", 1),
    ("unit", 0, 1, 0, 0), ("unit", 0, 1, 1, 0), ("cgrad", 0, 1, 0), ("fwd", 0, 1, 0),
    ("unit", 0, 1, 0, 1), ("unit", 0, 1, 0, 3), ("fwd", 0, 1, 1), ("unit", 0, 1, 1, 1),
    ("unit", 0, 1, 1, 3), ("cgrad", 0, 1, 1), ("relay", 2, 0), ("unit", 0, 1, 0, 2),
    ("relay", 2, 1), ("cgrad", 0, 1, 3), ("unit", 0, 1, 1, 2), ("cgrad", 0, 1, 2), ("con",),
    ("half", 0, 1, 0), ("half", 0, 1, 1), ("update", 1, 0), ("update", 1, 1), ("cin",),
    ("unit", 1, 1, 0, 0), ("unit", 1, 1, 1, 0), ("fwd", 1, 1, 0), ("unit", 1, 1, 0, 1),
    ("unit", 1, 1, 0, 3), ("fwd", 1, 1, 1), ("unit", 1, 1, 1, 1), ("unit", 1, 1, 1, 3),
    ("cgrad", 1, 1, 0), ("relay", 1, 0), ("unit", 1, 1, 0, 2), ("cgrad", 1, 1, 1),
    ("relay", 1, 1), ("cgrad", 1, 1, 3), ("unit", 1, 1, 1, 2), ("cgrad", 1, 1, 2),
    ("half", 1, 1, 0), ("half", 1, 1, 1), ("update", 0, 0), ("unit", 1, 0, 0, 0),
    ("update", 0, 1), ("unit", 1, 0, 1, 0), ("cgrad", 1, 0, 0), ("fwd", 1, 0, 0),
    ("unit", 1, 0, 0, 1), ("unit", 1, 0, 0, 3), ("fwd", 1, 0, 1), ("unit", 1, 0, 1, 1),
    ("unit", 1, 0, 1, 3), ("cgrad", 1, 0, 1), ("relay", 3, 0), ("unit", 1, 0, 0, 2),
    ("cgrad", 1, 0, 3), ("relay", 3, 1), ("unit", 1, 0, 1, 2), ("cgrad", 1, 0, 2), ("clast",),
    ("half", 1, 0, 0), ("half", 1, 0, 1), ("result", 0), ("cresult",), ("result", 1),
)


def with_bias_rows(full, dim, first):
    top = dim - dim % 8
    tail = full[top:]
    at = dim % 8
    bias = tail[at + first:at + first + 1]
    high = bias.astype(BF16).astype(F32)
    low = bias - high
    row = lax.broadcasted_iota(jnp.int32, tail.shape, 0)
    other = 2 - first
    tail = jnp.where(row == at + first, high, tail)
    tail = jnp.where(row == at + first + 1, low, tail)
    tail = jnp.where((row >= at + other) & (row <= at + other + 1), 1.0, tail)
    return jnp.concatenate([full[:top], tail], axis=0).astype(BF16)


def kernel(nb, dim, wv, wb, cv, cb, cnt, msk, ow, owb, oc, ocb,
           wv_in, wb_in, cv_in, cb_in, cnt_in, in_s,
           wbuf, psend, pbuf, hsend, hrecv, zbuf, hsum, wp, wacc, hp, hbf, hbt, hprev, gacc,
           cacc, csend, crecv, fsend, frecv, wgt, wtl, gbuf,
           ag_s, ag_r, rs_s, rs_r, z1_s, z1_r, z2_s, z2_r, cx_s, cx_r):
    b = lax.axis_index("blk")
    c = lax.axis_index("col")
    y = lax.div(c, 2)
    zh = lax.rem(c, 2)
    upper = lax.div(b, nb // 2)
    across = lax.rem(b + nb // 2, nb)
    z_col = (y * 2 + lax.rem(zh + upper, 2), y * 2 + lax.rem(zh + 1 - upper, 2))
    nxt = lax.rem(b + 1, nb)
    prv = lax.rem(b + nb - 1, nb)
    width = wv.shape[1]
    halves = width // SIDE
    top, at = dim - dim % 8, dim % 8

    def remote(src, dst, ssem, rsem, blk, col):
        return pltpu.make_async_remote_copy(
            src_ref=src, dst_ref=dst, send_sem=ssem, recv_sem=rsem,
            device_id=(blk, col), device_id_type=MESH)

    def y_of(k):
        return lax.rem(y + k, N_Y)

    def mate(k):
        return y_of(k) * 2 + zh

    def ag_copy(t, p, f, k):
        return remote(wbuf.at[t, p, y, f], wbuf.at[t, p, y, f],
                      ag_s.at[t, p, f, k], ag_r.at[t, p, f, y], b, mate(k))

    def ag_forward(t, p, f):
        ys, to = (y_of(3), 1) if f == 0 else (y_of(1), 3)
        return remote(wbuf.at[t, p, ys, f], wbuf.at[t, p, ys, f],
                      ag_s.at[t, p, f, 2], ag_r.at[t, p, f, ys], b, mate(to))

    def ag_wait(t, p, f, k):
        yk = y_of(k)
        remote(wbuf.at[t, p, yk, f], wbuf.at[t, p, yk, f],
               ag_s.at[t, p, f, k], ag_r.at[t, p, f, yk], b, mate(k)).wait_recv()

    def rs_copy(t, p, f, k):
        return remote(psend.at[t, p, y_of(k), f], pbuf.at[t, p, y, f],
                      rs_s.at[t, p, f, k], rs_r.at[t, p, f, y], b, mate(k))

    def rs_wait(t, p, f, k):
        yk = y_of(k)
        remote(psend.at[t, p, yk, f], pbuf.at[t, p, yk, f],
               rs_s.at[t, p, f, k], rs_r.at[t, p, f, yk], b, mate(k)).wait_recv()

    def z_ends(i, f):
        return ((wbuf.at[0, 0, y, f], wbuf.at[0, 1, y, f]),
                (hsend.at[0, 1, f], hrecv.at[0, 0, f]),
                (hsend.at[0, 0, f], hrecv.at[0, 1, f]),
                (hsend.at[1, 1, f], hrecv.at[1, 0, f]))[i]

    def z_first(i, f):
        return remote(z_ends(i, f)[0], zbuf.at[i, f], z1_s.at[i, f], z1_r.at[i, f], across, z_col[f])

    def z_second(i, f):
        return remote(zbuf.at[i, f], z_ends(i, f)[1], z2_s.at[i, f], z2_r.at[i, f],
                      across, z_col[f])

    def relay(i, f):
        z_first(i, f).wait_recv()
        z_second(i, f).start()

    def cx_copy(i):
        src, dst = ((hbf.at[0], hprev), (csend, crecv), (fsend, frecv))[i]
        return remote(src, dst, cx_s.at[i], cx_r.at[i], nxt, c)

    def all_gather(t, p, f):
        for k in ((1, 3) if f == 0 else (3, 1)):
            ag_copy(t, p, f, k).start()

    def shard_of(p, j):
        return y_of(j) * 2 + (zh if p == 0 else 1 - zh)

    def prep(t, p, f):
        def step(k, carry):
            tile_row = shard_of(p, k) * halves + f
            rows = pl.ds(pl.multiple_of(tile_row * SIDE, SIDE), SIDE)
            for q in range(halves):
                cols = pl.ds(q * SIDE, SIDE)
                logx = jnp.log(cnt_in[t, rows, cols].astype(F32).T)
                weight = jnp.minimum(jnp.exp(POWER * logx - POWER * math.log(XMAX)), 1.0)
                weight = weight * msk[t, q, tile_row].astype(F32)
                wgt[t, p, k, f, cols, :] = weight
                wtl[t, p, k, f, cols, :] = weight * jnp.maximum(logx, 0.0)
            return carry

        lax.fori_loop(0, N_Y, step, 0)

    def fwd(t, p, f):
        ag_wait(t, p, f, 3 if f == 0 else 1)
        ag_forward(t, p, f).start()

    def unit(t, p, f, k):
        if k == 2 or k == (1 if f == 0 else 3):
            ag_wait(t, p, f, k)
        yk = y_of(k)
        pred = jnp.dot(hbt[t], wbuf[t, p, yk, f], preferred_element_type=F32)
        g = (wgt[t, p, k, f] * pred - wtl[t, p, k, f]).astype(BF16)
        gbuf[t, p, k, :, f * SIDE:(f + 1) * SIDE] = g
        psend[t, p, yk, f] = jnp.dot(hbf[t], g, preferred_element_type=F32).astype(BF16)
        if k:
            rs_copy(t, p, f, k).start()

    def cgrad(t, p, k):
        yk = y_of(k)
        words = jnp.concatenate([wbuf[t, p, yk, f] for f in range(halves)], axis=1)
        gacc[t] += lax.dot_general(words, gbuf[t, p, k], (((1,), (1,)), ((), ())),
                                   preferred_element_type=F32)

    def half(t, p, f):
        total = psend[t, p, y, f].astype(F32)
        for k in (1, 3, 2):
            rs_wait(t, p, f, k)
            total = total + pbuf[t, p, y_of(k), f].astype(F32)
        hsum[t, p, f] = total
        if (t, p) != (1, 0):
            hsend[t, p, f] = total.astype(BF16)
            z_first({(0, 0): 2, (0, 1): 1, (1, 1): 3}[t, p], f).start()

    def partner_words(f):
        z_second(0, f).wait_recv()
        all_gather(0, 1, f)

    def update(p, f):
        z_second(1 + p, f).wait_recv()
        grad = hsum[0, p, f] + hrecv[0, p, f].astype(F32)
        acc = 1.0 + grad * grad
        words = wp[f] if p == 0 else with_whole_bias(wbuf[0, 1, y, f].astype(F32), 0)
        words = words - RATE * grad * lax.rsqrt(acc)
        if p == 0:
            wacc[f] = acc
            wp[f] = words
        wbuf[1, p, y, f] = with_bias_rows(words, dim, 0)
        all_gather(1, p, f)

    def result(f):
        z_second(3, f).wait_recv()
        grad = hsum[1, 0, f] + hrecv[1, 0, f].astype(F32)
        words = wp[f] - RATE * grad * lax.rsqrt(wacc[f] + grad * grad)
        lanes = slice(f * SIDE, (f + 1) * SIDE)
        ow[:, lanes] = words[0:dim]
        owb[:, lanes] = words[dim:dim + 1]

    def context_early():
        cx_copy(0).start()

    def context_on():
        csend[...] = gacc[0].astype(BF16)
        cx_copy(1).start()

    def context_in():
        cx_copy(0).wait_recv()
        cx_copy(1).wait_recv()
        grad = crecv[...].astype(F32)
        acc = 1.0 + grad * grad
        cacc[...] = acc
        held = with_whole_bias(hprev[...].astype(F32), 2) - RATE * grad * lax.rsqrt(acc)
        hp[...] = held
        hbf[1] = with_bias_rows(held, dim, 2)
        hbt[1] = hbf[1].astype(F32).T.astype(BF16)

    def context_last():
        grad = gacc[1]
        held = hp[...] - RATE * grad * lax.rsqrt(cacc[...] + grad * grad)
        fsend[...] = with_bias_rows(held, dim, 2)
        cx_copy(2).start()

    def context_result():
        cx_copy(2).wait_recv()
        held = frecv[...].astype(F32)
        oc[...] = held[0:dim]
        ocb[...] = held[dim + 2:dim + 3] + held[dim + 3:dim + 4]

    def with_whole_bias(full, first):
        end = full[top:]
        i = at + first
        row = lax.broadcasted_iota(jnp.int32, end.shape, 0)
        end = jnp.where(row == i, end[i:i + 1] + end[i + 1:i + 2], end)
        return jnp.concatenate([full[:top], end], axis=0)

    barrier = pltpu.get_barrier_semaphore()
    others = [(b, mate(k)) for k in (1, 2, 3)] + [
        (across, z_col[0]), (across, z_col[1]), (nxt, c), (prv, c)]
    for other in others:
        pl.semaphore_signal(barrier, inc=1, device_id=other, device_id_type=MESH)

    loads = [pltpu.make_async_copy(src, dst, in_s.at[i]) for i, (src, dst) in enumerate(
        ((wv, wv_in), (wb, wb_in), (cnt, cnt_in), (cv, cv_in), (cb, cb_in)))]
    for load in loads:
        load.start()

    loads[0].wait()
    loads[1].wait()
    for f in range(halves):
        lanes = slice(f * SIDE, (f + 1) * SIDE)
        wp[f, 0:dim, :] = wv_in[:, lanes]
        wp[f, dim:dim + 1, :] = wb_in[:, lanes]
        wp[f, dim + 1:dim + 4, :] = jnp.zeros((3, SIDE), F32)
        wbuf[0, 0, y, f] = with_bias_rows(wp[f], dim, 0)

    pl.semaphore_wait(barrier, len(others))

    for f in range(halves):
        z_first(0, f).start()
        all_gather(0, 0, f)
    for load in loads[2:]:
        load.wait()
    hp[0:dim, :] = cv_in[...]
    hp[dim:dim + 2, :] = jnp.zeros((2, width), F32)
    hp[dim + 2:dim + 3, :] = cb_in[...]
    hp[dim + 3:dim + 4, :] = jnp.zeros((1, width), F32)
    hbf[0] = with_bias_rows(hp[...], dim, 2)
    hbt[0] = hbf[0].astype(F32).T.astype(BF16)
    gacc[...] = jnp.zeros_like(gacc)

    steps = dict(relay=relay, prep=prep, unit=unit, fwd=fwd, half=half, cgrad=cgrad, words=partner_words,
                 update=update, result=result, cearly=context_early, con=context_on, cin=context_in,
                 clast=context_last, cresult=context_result)
    for name, *which in ORDER:
        steps[name](*which)

    for f in range(halves):
        for i in range(4):
            z_first(i, f).wait_send()
            z_second(i, f).wait_send()
        for t in range(2):
            for p in range(2):
                ag_forward(t, p, f).wait_send()
                ag_copy(t, p, f, 1).wait_send()
                ag_copy(t, p, f, 3).wait_send()
                for k in (1, 2, 3):
                    rs_copy(t, p, f, k).wait_send()
    for i in range(3):
        cx_copy(i).wait_send()


def copy_out(*refs):
    n = len(refs) // 2
    sems = refs[-1]
    copies = [pltpu.make_async_copy(refs[i], refs[n + i], sems.at[i]) for i in range(n)]
    for copy in copies:
        copy.start()
    for copy in copies:
        copy.wait()


def per_device(nb, word_vectors, word_bias, context_vectors, context_bias, counts, tile_mask):
    dim, width = word_vectors.shape
    tall, halves = dim + 4, width // SIDE
    vmem = pl.BlockSpec(memory_space=pltpu.VMEM)
    hbm = pl.BlockSpec(memory_space=pltpu.HBM)
    dma = pltpu.SemaphoreType.DMA
    piece = (halves, tall, SIDE)
    shapes = tuple(pltpu.VMEM((n, width), F32) for n in (dim, 1, dim, 1))
    results = pl.pallas_call(
        functools.partial(kernel, nb, dim),
        out_shape=shapes,
        in_specs=[hbm] * 5 + [pl.BlockSpec(memory_space=pltpu.SMEM)],
        out_specs=(vmem,) * 4,
        scratch_shapes=[
            pltpu.VMEM((dim, width), F32),
            pltpu.VMEM((1, width), F32),
            pltpu.VMEM((dim, width), F32),
            pltpu.VMEM((1, width), F32),
            pltpu.VMEM(counts.shape, BF16),
            dma((5,)),
            pltpu.VMEM((2, 2, N_Y) + piece, BF16),
            pltpu.VMEM((2, 2, N_Y) + piece, BF16),
            pltpu.VMEM((2, 2, N_Y) + piece, BF16),
            pltpu.VMEM((2, 2) + piece, BF16),
            pltpu.VMEM((2, 2) + piece, BF16),
            pltpu.VMEM((4,) + piece, BF16),
            pltpu.VMEM((2, 2) + piece, F32),
            pltpu.VMEM(piece, F32),
            pltpu.VMEM(piece, F32),
            pltpu.VMEM((tall, width), F32),
            pltpu.VMEM((2, tall, width), BF16),
            pltpu.VMEM((2, width, tall), BF16),
            pltpu.VMEM((tall, width), BF16),
            pltpu.VMEM((2, tall, width), F32),
            pltpu.VMEM((tall, width), F32),
            pltpu.VMEM((tall, width), BF16),
            pltpu.VMEM((tall, width), BF16),
            pltpu.VMEM((tall, width), BF16),
            pltpu.VMEM((tall, width), BF16),
            pltpu.VMEM((2, 2, N_Y, halves, width, SIDE), F32),
            pltpu.VMEM((2, 2, N_Y, halves, width, SIDE), F32),
            pltpu.VMEM((2, 2, N_Y, width, width), BF16),
            dma((2, 2, halves, N_Y)), dma((2, 2, halves, N_Y)),
            dma((2, 2, halves, N_Y)), dma((2, 2, halves, N_Y)),
            dma((4, halves)), dma((4, halves)),
            dma((4, halves)), dma((4, halves)),
            dma((3,)), dma((3,)),
        ],
        compiler_params=pltpu.CompilerParams(
            collective_id=0, has_side_effects=True, vmem_limit_bytes=60 * 1024 * 1024),
        cost_estimate=pl.CostEstimate(
            flops=2 * 6 * tall * counts.shape[1] * width, transcendentals=2 * counts.size,
            bytes_accessed=2 * counts.size + 16 * dim * width),
    )(word_vectors, word_bias[None], context_vectors, context_bias[None], counts,
      tile_mask.transpose(0, 2, 1))
    ow, owb, oc, ocb = pl.pallas_call(
        copy_out, out_shape=tuple(jax.ShapeDtypeStruct(s.shape, F32) for s in shapes),
        in_specs=[vmem] * 4, out_specs=(hbm,) * 4,
        scratch_shapes=[dma((4,))],
        compiler_params=pltpu.CompilerParams(vmem_limit_bytes=4 * 1024 * 1024),
        cost_estimate=pl.CostEstimate(
            flops=0, transcendentals=0, bytes_accessed=16 * dim * width),
    )(*results)
    return ow, owb[0], oc, ocb[0]


def solution(mesh):
    spec = P(None, ("blk", "col"))
    line = P(("blk", "col"))
    grid = P(None, "blk", "col")
    return jax.shard_map(
        functools.partial(per_device, mesh.shape["blk"]), mesh=mesh,
        in_specs=(spec, line, spec, line, grid, grid),
        out_specs=(spec, line, spec, line), check_vma=False)
```

```python
import functools
import math

import jax
import jax.numpy as jnp
from jax import lax
from jax.experimental import pallas as pl
from jax.experimental.pallas import tpu as pltpu
from jax.sharding import PartitionSpec as P

RATE = 0.05
XMAX = 100.0
POWER = 0.75
MESH = pl.DeviceIdType.MESH
F32 = jnp.float32
BF16 = jnp.bfloat16
N_Y = 4
SIDE = 128

ORDER = (
    ("cearly",), ("prep", 0, 0, 0), ("prep", 0, 0, 1), ("prep", 0, 1, 0), ("fwd", 0, 0, 0),
    ("near", 0, 0, 0), ("fwd", 0, 0, 1), ("near", 0, 0, 1), ("cgrad", 0, 0, 0, 0),
    ("far", 0, 0, 0), ("relay", 0, 0), ("relay", 0, 1), ("cgrad", 0, 0, 1, 0),
    ("cgrad", 0, 0, 0, 1), ("prep", 0, 1, 1), ("far", 0, 0, 1), ("cgrad", 0, 0, 1, 1),
    ("prep", 1, 1, 0), ("prep", 1, 1, 1), ("half", 0, 0, 0), ("prep", 1, 0, 0), ("half", 0, 0, 1),
    ("words", 0), ("words", 1), ("prep", 1, 0, 1), ("fwd", 0, 1, 0), ("near", 0, 1, 0),
    ("cgrad", 0, 1, 0, 0), ("fwd", 0, 1, 1), ("near", 0, 1, 1), ("relay", 2, 0), ("far", 0, 1, 0),
    ("relay", 2, 1), ("cgrad", 0, 1, 1, 0), ("cgrad", 0, 1, 0, 1), ("far", 0, 1, 1),
    ("cgrad", 0, 1, 1, 1), ("con",), ("half", 0, 1, 0), ("update", 1, 0), ("half", 0, 1, 1),
    ("update", 1, 1), ("drain", 0, 0), ("fwd", 1, 1, 0), ("cin",), ("near", 1, 1, 0),
    ("fwd", 1, 1, 1), ("near", 1, 1, 1), ("relay", 1, 0), ("far", 1, 1, 0), ("relay", 1, 1),
    ("cgrad", 1, 1, 0, 0), ("cgrad", 1, 1, 1, 0), ("cgrad", 1, 1, 0, 1), ("far", 1, 1, 1),
    ("cgrad", 1, 1, 1, 1), ("half", 1, 1, 0), ("update", 0, 0), ("half", 1, 1, 1),
    ("update", 0, 1), ("drain", 0, 1), ("fwd", 1, 0, 0), ("near", 1, 0, 0), ("cgrad", 1, 0, 0, 0),
    ("fwd", 1, 0, 1), ("near", 1, 0, 1), ("far", 1, 0, 0), ("relay", 3, 0), ("cgrad", 1, 0, 1, 0),
    ("cgrad", 1, 0, 0, 1), ("relay", 3, 1), ("far", 1, 0, 1), ("cgrad", 1, 0, 1, 1), ("clast",),
    ("drain", 1, 1), ("half", 1, 0, 0), ("half", 1, 0, 1), ("drain", 1, 0), ("result", 0),
    ("cresult",), ("result", 1),
)


def with_bias_rows(full, dim, first):
    top = dim - dim % 8
    tail = full[top:]
    at = dim % 8
    bias = tail[at + first:at + first + 1]
    high = bias.astype(BF16).astype(F32)
    low = bias - high
    row = lax.broadcasted_iota(jnp.int32, tail.shape, 0)
    other = 2 - first
    tail = jnp.where(row == at + first, high, tail)
    tail = jnp.where(row == at + first + 1, low, tail)
    tail = jnp.where((row >= at + other) & (row <= at + other + 1), 1.0, tail)
    return jnp.concatenate([full[:top], tail], axis=0).astype(BF16)


def kernel(nb, dim, wv, wb, cv, cb, cnt, msk, ow, owb, oc, ocb,
           wv_in, wb_in, cv_in, cb_in, cnt_in, in_s,
           wbuf, psend, pbuf, hsend, hrecv, zbuf, hsum, wp, wacc, hp, hbf, hbt, hprev, gacc,
           cacc, csend, crecv, fsend, frecv, wgt, wtl, gbuf,
           ag_s, ag_r, rs_s, rs_r, z1_s, z1_r, z2_s, z2_r, cx_s, cx_r):
    b = lax.axis_index("blk")
    c = lax.axis_index("col")
    y = lax.div(c, 2)
    zh = lax.rem(c, 2)
    upper = lax.div(b, nb // 2)
    across = lax.rem(b + nb // 2, nb)
    z_col = (y * 2 + lax.rem(zh + upper, 2), y * 2 + lax.rem(zh + 1 - upper, 2))
    nxt = lax.rem(b + 1, nb)
    prv = lax.rem(b + nb - 1, nb)
    width = wv.shape[1]
    halves = width // SIDE
    top, at = dim - dim % 8, dim % 8

    def remote(src, dst, ssem, rsem, blk, col):
        return pltpu.make_async_remote_copy(
            src_ref=src, dst_ref=dst, send_sem=ssem, recv_sem=rsem,
            device_id=(blk, col), device_id_type=MESH)

    def y_of(k):
        return lax.rem(y + k, N_Y)

    def mate(k):
        return y_of(k) * 2 + zh

    def ag_copy(t, p, f, k):
        return remote(wbuf.at[t, p, y, f], wbuf.at[t, p, y, f],
                      ag_s.at[t, p, f, k], ag_r.at[t, p, f, y], b, mate(k))

    def ag_forward(t, p, f):
        ys, to = (y_of(3), 1) if f == 0 else (y_of(1), 3)
        return remote(wbuf.at[t, p, ys, f], wbuf.at[t, p, ys, f],
                      ag_s.at[t, p, f, 2], ag_r.at[t, p, f, ys], b, mate(to))

    def ag_wait(t, p, f, k):
        yk = y_of(k)
        remote(wbuf.at[t, p, yk, f], wbuf.at[t, p, yk, f],
               ag_s.at[t, p, f, k], ag_r.at[t, p, f, yk], b, mate(k)).wait_recv()

    def rs_copy(t, p, f, k):
        return remote(psend.at[t, p, y_of(k), f], pbuf.at[t, p, y, f],
                      rs_s.at[t, p, f, k], rs_r.at[t, p, f, y], b, mate(k))

    def rs_wait(t, p, f, k):
        yk = y_of(k)
        remote(psend.at[t, p, yk, f], pbuf.at[t, p, yk, f],
               rs_s.at[t, p, f, k], rs_r.at[t, p, f, yk], b, mate(k)).wait_recv()

    def z_ends(i, f):
        return ((wbuf.at[0, 0, y, f], wbuf.at[0, 1, y, f]),
                (hsend.at[0, 1, f], hrecv.at[0, 0, f]),
                (hsend.at[0, 0, f], hrecv.at[0, 1, f]),
                (hsend.at[1, 1, f], hrecv.at[1, 0, f]))[i]

    def z_first(i, f):
        return remote(z_ends(i, f)[0], zbuf.at[i, f], z1_s.at[i, f], z1_r.at[i, f], across, z_col[f])

    def z_second(i, f):
        return remote(zbuf.at[i, f], z_ends(i, f)[1], z2_s.at[i, f], z2_r.at[i, f],
                      across, z_col[f])

    def relay(i, f):
        z_first(i, f).wait_recv()
        z_second(i, f).start()

    def cx_copy(i):
        src, dst = ((hbf.at[0], hprev), (csend, crecv), (fsend, frecv))[i]
        return remote(src, dst, cx_s.at[i], cx_r.at[i], nxt, c)

    def all_gather(t, p, f):
        for k in ((1, 3) if f == 0 else (3, 1)):
            ag_copy(t, p, f, k).start()

    def shard_of(p, j):
        return y_of(j) * 2 + (zh if p == 0 else 1 - zh)

    def prep(t, p, f):
        def step(k, carry):
            tile_row = shard_of(p, k) * halves + f
            rows = pl.ds(pl.multiple_of(tile_row * SIDE, SIDE), SIDE)
            for q in range(halves):
                cols = pl.ds(q * SIDE, SIDE)
                logx = jnp.log(cnt_in[t, rows, cols].astype(F32).T)
                weight = jnp.minimum(jnp.exp(POWER * logx - POWER * math.log(XMAX)), 1.0)
                weight = weight * msk[t, q, tile_row].astype(F32)
                wgt[t, p, k, f, cols, :] = weight
                wtl[t, p, k, f, cols, :] = weight * jnp.maximum(logx, 0.0)
            return carry

        lax.fori_loop(0, N_Y, step, 0)

    def fwd(t, p, f):
        ag_wait(t, p, f, 3 if f == 0 else 1)
        ag_forward(t, p, f).start()

    def pair(t, p, f, ks):
        return jnp.concatenate([wbuf[t, p, y_of(k), f] for k in ks], axis=1)

    def products(t, p, f, ks):
        both = [jnp.concatenate([ref[t, p, k, f] for k in ks], axis=1) for ref in (wgt, wtl)]
        pred = jnp.dot(hbt[t], pair(t, p, f, ks), preferred_element_type=F32)
        g = (both[0] * pred - both[1]).astype(BF16)
        gbuf[t, p, f, int(0 in ks)] = g
        part = jnp.dot(hbf[t], g, preferred_element_type=F32).astype(BF16)
        for i, k in enumerate(ks):
            psend[t, p, y_of(k), f] = part[:, i * SIDE:(i + 1) * SIDE]
            if k:
                rs_copy(t, p, f, k).start()

    def near(t, p, f):
        ag_wait(t, p, f, 1 if f == 0 else 3)
        products(t, p, f, (1, 3))

    def far(t, p, f):
        ag_wait(t, p, f, 2)
        products(t, p, f, (2, 0))

    def cgrad(t, p, f, i):
        words = pair(t, p, f, ((1, 3), (2, 0))[i])
        gacc[t] += lax.dot_general(words, gbuf[t, p, f, i], (((1,), (1,)), ((), ())),
                                   preferred_element_type=F32)

    def drain(t, p):
        for f in range(halves):
            ag_forward(t, p, f).wait_send()
            ag_copy(t, p, f, 1).wait_send()
            ag_copy(t, p, f, 3).wait_send()
            for k in (1, 2, 3):
                rs_copy(t, p, f, k).wait_send()

    def half(t, p, f):
        total = psend[t, p, y, f].astype(F32)
        for k in (1, 3, 2):
            rs_wait(t, p, f, k)
            total = total + pbuf[t, p, y_of(k), f].astype(F32)
        hsum[t, p, f] = total
        if (t, p) != (1, 0):
            hsend[t, p, f] = total.astype(BF16)
            z_first({(0, 0): 2, (0, 1): 1, (1, 1): 3}[t, p], f).start()

    def partner_words(f):
        z_second(0, f).wait_recv()
        all_gather(0, 1, f)

    def update(p, f):
        z_second(1 + p, f).wait_recv()
        grad = hsum[0, p, f] + hrecv[0, p, f].astype(F32)
        acc = 1.0 + grad * grad
        words = wp[f] if p == 0 else with_whole_bias(wbuf[0, 1, y, f].astype(F32), 0)
        words = words - RATE * grad * lax.rsqrt(acc)
        if p == 0:
            wacc[f] = acc
            wp[f] = words
        wbuf[1, p, y, f] = with_bias_rows(words, dim, 0)
        all_gather(1, p, f)

    def result(f):
        z_second(3, f).wait_recv()
        grad = hsum[1, 0, f] + hrecv[1, 0, f].astype(F32)
        words = wp[f] - RATE * grad * lax.rsqrt(wacc[f] + grad * grad)
        lanes = slice(f * SIDE, (f + 1) * SIDE)
        ow[:, lanes] = words[0:dim]
        owb[:, lanes] = words[dim:dim + 1]

    def context_early():
        cx_copy(0).start()

    def context_on():
        csend[...] = gacc[0].astype(BF16)
        cx_copy(1).start()

    def context_in():
        cx_copy(0).wait_recv()
        cx_copy(1).wait_recv()
        grad = crecv[...].astype(F32)
        acc = 1.0 + grad * grad
        cacc[...] = acc
        held = with_whole_bias(hprev[...].astype(F32), 2) - RATE * grad * lax.rsqrt(acc)
        hp[...] = held
        hbf[1] = with_bias_rows(held, dim, 2)
        hbt[1] = hbf[1].astype(F32).T.astype(BF16)

    def context_last():
        grad = gacc[1]
        held = hp[...] - RATE * grad * lax.rsqrt(cacc[...] + grad * grad)
        fsend[...] = with_bias_rows(held, dim, 2)
        cx_copy(2).start()

    def context_result():
        cx_copy(2).wait_recv()
        held = frecv[...].astype(F32)
        oc[...] = held[0:dim]
        ocb[...] = held[dim + 2:dim + 3] + held[dim + 3:dim + 4]

    def with_whole_bias(full, first):
        end = full[top:]
        i = at + first
        row = lax.broadcasted_iota(jnp.int32, end.shape, 0)
        end = jnp.where(row == i, end[i:i + 1] + end[i + 1:i + 2], end)
        return jnp.concatenate([full[:top], end], axis=0)

    barrier = pltpu.get_barrier_semaphore()
    others = [(b, mate(k)) for k in (1, 2, 3)] + [
        (across, z_col[0]), (across, z_col[1]), (nxt, c), (prv, c)]
    for other in others:
        pl.semaphore_signal(barrier, inc=1, device_id=other, device_id_type=MESH)

    loads = [pltpu.make_async_copy(src, dst, in_s.at[i]) for i, (src, dst) in enumerate(
        ((wv, wv_in), (wb, wb_in), (cnt, cnt_in), (cv, cv_in), (cb, cb_in)))]
    for load in loads:
        load.start()

    loads[0].wait()
    loads[1].wait()
    for f in range(halves):
        lanes = slice(f * SIDE, (f + 1) * SIDE)
        wp[f, 0:dim, :] = wv_in[:, lanes]
        wp[f, dim:dim + 1, :] = wb_in[:, lanes]
        wp[f, dim + 1:dim + 4, :] = jnp.zeros((3, SIDE), F32)
        wbuf[0, 0, y, f] = with_bias_rows(wp[f], dim, 0)

    pl.semaphore_wait(barrier, len(others))

    for f in range(halves):
        z_first(0, f).start()
        all_gather(0, 0, f)
    for load in loads[2:]:
        load.wait()
    hp[0:dim, :] = cv_in[...]
    hp[dim:dim + 2, :] = jnp.zeros((2, width), F32)
    hp[dim + 2:dim + 3, :] = cb_in[...]
    hp[dim + 3:dim + 4, :] = jnp.zeros((1, width), F32)
    hbf[0] = with_bias_rows(hp[...], dim, 2)
    hbt[0] = hbf[0].astype(F32).T.astype(BF16)
    gacc[...] = jnp.zeros_like(gacc)

    steps = dict(relay=relay, prep=prep, near=near, far=far, fwd=fwd, drain=drain, half=half, cgrad=cgrad, words=partner_words,
                 update=update, result=result, cearly=context_early, con=context_on, cin=context_in,
                 clast=context_last, cresult=context_result)
    for name, *which in ORDER:
        steps[name](*which)

    for f in range(halves):
        for i in range(4):
            z_first(i, f).wait_send()
            z_second(i, f).wait_send()
    for i in range(3):
        cx_copy(i).wait_send()


def copy_out(*refs):
    n = len(refs) // 2
    sems = refs[-1]
    copies = [pltpu.make_async_copy(refs[i], refs[n + i], sems.at[i]) for i in range(n)]
    for copy in copies:
        copy.start()
    for copy in copies:
        copy.wait()


def per_device(nb, word_vectors, word_bias, context_vectors, context_bias, counts, tile_mask):
    dim, width = word_vectors.shape
    tall, halves = dim + 4, width // SIDE
    vmem = pl.BlockSpec(memory_space=pltpu.VMEM)
    hbm = pl.BlockSpec(memory_space=pltpu.HBM)
    dma = pltpu.SemaphoreType.DMA
    piece = (halves, tall, SIDE)
    shapes = tuple(pltpu.VMEM((n, width), F32) for n in (dim, 1, dim, 1))
    results = pl.pallas_call(
        functools.partial(kernel, nb, dim),
        out_shape=shapes,
        in_specs=[hbm] * 5 + [pl.BlockSpec(memory_space=pltpu.SMEM)],
        out_specs=(vmem,) * 4,
        scratch_shapes=[
            pltpu.VMEM((dim, width), F32),
            pltpu.VMEM((1, width), F32),
            pltpu.VMEM((dim, width), F32),
            pltpu.VMEM((1, width), F32),
            pltpu.VMEM(counts.shape, BF16),
            dma((5,)),
            pltpu.VMEM((2, 2, N_Y) + piece, BF16),
            pltpu.VMEM((2, 2, N_Y) + piece, BF16),
            pltpu.VMEM((2, 2, N_Y) + piece, BF16),
            pltpu.VMEM((2, 2) + piece, BF16),
            pltpu.VMEM((2, 2) + piece, BF16),
            pltpu.VMEM((4,) + piece, BF16),
            pltpu.VMEM((2, 2) + piece, F32),
            pltpu.VMEM(piece, F32),
            pltpu.VMEM(piece, F32),
            pltpu.VMEM((tall, width), F32),
            pltpu.VMEM((2, tall, width), BF16),
            pltpu.VMEM((2, width, tall), BF16),
            pltpu.VMEM((tall, width), BF16),
            pltpu.VMEM((2, tall, width), F32),
            pltpu.VMEM((tall, width), F32),
            pltpu.VMEM((tall, width), BF16),
            pltpu.VMEM((tall, width), BF16),
            pltpu.VMEM((tall, width), BF16),
            pltpu.VMEM((tall, width), BF16),
            pltpu.VMEM((2, 2, N_Y, halves, width, SIDE), F32),
            pltpu.VMEM((2, 2, N_Y, halves, width, SIDE), F32),
            pltpu.VMEM((2, 2, halves, 2, width, 2 * SIDE), BF16),
            dma((2, 2, halves, N_Y)), dma((2, 2, halves, N_Y)),
            dma((2, 2, halves, N_Y)), dma((2, 2, halves, N_Y)),
            dma((4, halves)), dma((4, halves)),
            dma((4, halves)), dma((4, halves)),
            dma((3,)), dma((3,)),
        ],
        compiler_params=pltpu.CompilerParams(
            collective_id=0, has_side_effects=True, vmem_limit_bytes=60 * 1024 * 1024),
        cost_estimate=pl.CostEstimate(
            flops=2 * 6 * tall * counts.shape[1] * width, transcendentals=2 * counts.size,
            bytes_accessed=2 * counts.size + 16 * dim * width),
    )(word_vectors, word_bias[None], context_vectors, context_bias[None], counts,
      tile_mask.transpose(0, 2, 1))
    ow, owb, oc, ocb = pl.pallas_call(
        copy_out, out_shape=tuple(jax.ShapeDtypeStruct(s.shape, F32) for s in shapes),
        in_specs=[vmem] * 4, out_specs=(hbm,) * 4,
        scratch_shapes=[dma((4,))],
        compiler_params=pltpu.CompilerParams(vmem_limit_bytes=4 * 1024 * 1024),
        cost_estimate=pl.CostEstimate(
            flops=0, transcendentals=0, bytes_accessed=16 * dim * width),
    )(*results)
    return ow, owb[0], oc, ocb[0]


def solution(mesh):
    spec = P(None, ("blk", "col"))
    line = P(("blk", "col"))
    grid = P(None, "blk", "col")
    return jax.shard_map(
        functools.partial(per_device, mesh.shape["blk"]), mesh=mesh,
        in_specs=(spec, line, spec, line, grid, grid),
        out_specs=(spec, line, spec, line), check_vma=False)
```
